128 devices in a mesh: fsdp: 4 (over z), seq: 32 (over x, y, core).
Axes of the slice: x: 4, y: 4, z: 4, core: 2. Of those that a mesh axis runs over, the one named last changes fastest.
Arguments:
- patches: bfloat16 [128, 256, 1536], P(('fsdp', 'seq')), may hold values from -6 to 6
- gain_tile: float32 [1536], replicated, may hold values from 0.1 to 1.9
- w_kv: bfloat16 [1536, 3072], P(None, ('fsdp', 'seq')), may hold values from -2 to 2
- w_q: bfloat16 [1536, 1536], P(None, ('fsdp', 'seq')), may hold values from -2 to 2
- w_to: bfloat16 [1536, 1536], P(None, ('fsdp', 'seq')), may hold values from -0.15625 to 0.15625
- gain_final: float32 [1536], replicated, may hold values from 0.1 to 1.9
- w_proj: bfloat16 [1536, 768], P(None, ('fsdp', 'seq')), may hold values from -0.15625 to 0.15625
- positions: int32 [128], P('fsdp'), may hold values from 0 to 32767, as said below
- counts: int32 [4], P('fsdp'), may hold values from 8192 to 32768, as said below
- cache: bfloat16 [4, 32768, 768], P('fsdp', 'seq'), may hold values from -6 to 6
- gain_slide: float32 [768], replicated, may hold values from 0.1 to 1.9
- w_slide_qkv: bfloat16 [768, 2304], replicated, may hold values from -2 to 2
- w_slide_out: bfloat16 [768, 768], replicated, may hold values from -0.21875 to 0.21875
Outputs:
- encoded: bfloat16 [4, 32768, 768], P('fsdp', 'seq')
The draws below stay inside these ranges and needn't reach their ends.
Inputs may be any that keep to these rules, and one draw needn't show every extreme that they name: Slide k holds tissue at its first counts[k] positions; one slide is full and another has exactly a quarter of 32768. `positions`: entries k * 32 to (k + 1) * 32 - 1 belong to slide k; they are distinct and below counts[k], and include 0 and counts[k] - 1.
All inputs are finite; a program needn't handle non-finite values.
Results may differ from the reference program's by a relative error of at most 0.008.
The reference program's roundings to bfloat16 on the way count: a program that leaves them out, or rounds other values in their place, can miss the bound.
Values may be sent and summed in bfloat16 or wider, within the bound.
A program may use at most 192 MiB of HBM per device.

```python
import math
import jax
import jax.numpy as jnp
from jax import lax

W = 1536
HEAD_T = 64
HEADS_T = 24
P_SIZE = 256
TILE_DEV = 1
TILES = 128
E = 768
HEADS_S = 16
HEAD_S = 48
SLIDE_LEN = 32768
SLIDES = 4
NEW_SLIDE = 32
SEG = 1024
RATE = 16


def tissue_counts(key):
    key = jax.random.fold_in(key, 11)
    first_key, second = jax.random.split(key)
    draws_int = jax.random.randint(first_key, (SLIDES,), SLIDE_LEN // 4, SLIDE_LEN + 1)
    ranking = jax.random.permutation(second, SLIDES)
    draws_int = jnp.where(ranking == 0, SLIDE_LEN, draws_int)
    draws_int = jnp.where(ranking == 1, SLIDE_LEN // 4, draws_int)
    return draws_int.astype(jnp.int32)


def column_levels(key, head_count, top_level, salt):
    key = jax.random.fold_in(key, salt)
    first_key, second = jax.random.split(key)
    levels = jax.random.uniform(first_key, (head_count,), jnp.float32)
    ranking = jax.random.permutation(second, head_count)
    levels = jnp.where(ranking == 0, 1.0, levels)
    levels = jnp.where(ranking == 1, 0.0, levels)
    return jnp.sqrt(top_level ** levels).astype(jnp.float32)


def draw_counts(key, part):
    return tissue_counts(key)


def draw_positions(key, part):
    tissue = tissue_counts(key)
    key = jax.random.fold_in(key, 5)
    top_value = 2 ** 31 // SLIDE_LEN - 1
    draws_int = jax.random.randint(key, (SLIDES, SLIDE_LEN), 0, top_value)
    places = jnp.arange(SLIDE_LEN, dtype=jnp.int32)
    forced = (places[None, :] == 0) | (places[None, :] == tissue[:, None] - 1)
    draws_int = jnp.where(forced, top_value, draws_int)
    scores = draws_int * SLIDE_LEN + places[None, :]
    scores = jnp.where(places[None, :] < tissue[:, None], scores, -1)
    chosen = lax.top_k(scores, NEW_SLIDE)[1]
    return chosen.reshape(SLIDES * NEW_SLIDE).astype(jnp.int32)


def draw_w_q(key, part):
    factors = column_levels(key, HEADS_T, 1.0, 23)
    key = jax.random.fold_in(key, 31)
    column_scale = jnp.repeat(factors, HEAD_T)
    entries = jnp.clip(jax.random.normal(key, (W, W), jnp.float32), -6.0, 6.0)
    return (entries * column_scale[None, :] / math.sqrt(W)).astype(jnp.bfloat16)


def draw_w_kv(key, part):
    factors = column_levels(key, HEADS_T, 1.0, 23)
    key = jax.random.fold_in(key, 37)
    column_scale = jnp.concatenate([jnp.repeat(factors, HEAD_T), jnp.ones((W,), jnp.float32)])
    entries = jnp.clip(jax.random.normal(key, (W, 2 * W), jnp.float32), -6.0, 6.0)
    return (entries * column_scale[None, :] / math.sqrt(W)).astype(jnp.bfloat16)


def draw_w_slide_qkv(key, part):
    factors = column_levels(key, HEADS_S, 1.0, 29)
    key = jax.random.fold_in(key, 41)
    spread_cols = jnp.repeat(factors, HEAD_S)
    column_scale = jnp.concatenate([spread_cols, spread_cols, jnp.ones((E,), jnp.float32)])
    entries = jnp.clip(jax.random.normal(key, (E, 3 * E), jnp.float32), -6.0, 6.0)
    return (entries * column_scale[None, :] / math.sqrt(E)).astype(jnp.bfloat16)


def shard_levels(key, dims, cuts, smallest, largest):
    gain = 1.0
    for dim, blocks in cuts:
        heights = jax.random.uniform(jax.random.fold_in(jax.random.fold_in(key, 6), dim), (blocks,), jnp.float32, smallest / len(cuts), largest / len(cuts))
        gain = gain * jnp.repeat(jnp.exp(heights), dims[dim] // blocks).reshape((-1,) + (1,) * (len(dims) - 1 - dim))
    return gain


def noise(key, dims, deviation, reach, pieces=(), kind=jnp.bfloat16):
    drawn = jax.random.normal(key, dims, jnp.float32) * deviation
    if len(pieces) > 0:
        drawn = shard_levels(key, dims, pieces, -0.22, 0.18) * drawn
    return jnp.clip(drawn, min=-reach, max=reach).astype(kind)


def setup_inputs(seed: int = 0) -> dict:
    splits = jax.random.split(jax.random.key(seed), 14)
    patches = noise(splits[0], (TILES, P_SIZE, W), 1.0, 6.0, ((0, 128),))
    gain_tile = jnp.clip(1.0 + 0.18 * jax.random.normal(splits[1], (W,), jnp.float32), 0.1, 1.9)
    w_kv = draw_w_kv(jax.random.fold_in(splits[13], 71), 0)
    w_q = draw_w_q(jax.random.fold_in(splits[13], 71), 0)
    w_to = noise(splits[4], (W, W), W ** -0.5, 0.15625, ((1, 128),))
    gain_final = jnp.clip(1.0 + 0.18 * jax.random.normal(splits[5], (W,), jnp.float32), 0.1, 1.9)
    w_proj = noise(splits[6], (W, E), W ** -0.5, 0.15625, ((1, 128),))
    positions = draw_positions(jax.random.fold_in(splits[13], 71), 0)
    counts = draw_counts(jax.random.fold_in(splits[13], 71), 0)
    cache = noise(splits[9], (SLIDES, SLIDE_LEN, E), 1.0, 6.0, ((0, 4), (1, 32)))
    gain_slide = jnp.clip(1.0 + 0.18 * jax.random.normal(splits[10], (E,), jnp.float32), 0.1, 1.9)
    w_slide_qkv = draw_w_slide_qkv(jax.random.fold_in(splits[13], 71), 0)
    w_slide_out = noise(splits[12], (E, E), E ** -0.5, 0.21875)
    return dict(patches=patches, gain_tile=gain_tile, w_kv=w_kv, w_q=w_q, w_to=w_to, gain_final=gain_final, w_proj=w_proj, positions=positions, counts=counts, cache=cache, gain_slide=gain_slide, w_slide_qkv=w_slide_qkv, w_slide_out=w_slide_out)


epsilon = 1e-06
masked = -1e+30
head_group = 4

def normalize(values, gain_vec):
    row_mean = lax.optimization_barrier(jnp.mean(values, -1, keepdims=True))
    centered = values - row_mean
    variance = lax.optimization_barrier(jnp.mean(centered * centered, -1, keepdims=True))
    return centered * lax.rsqrt(variance + epsilon) * gain_vec

def attend(queries, key_rows, value_rows, key_live, score_scale):
    scores = jnp.einsum('hrd,hkd->hrk', queries.astype(jnp.float32), key_rows.astype(jnp.float32)) * score_scale
    scores = jnp.where(key_live[:, None, :], scores, masked)
    row_max = lax.optimization_barrier(jnp.max(scores, -1))
    weights = jnp.exp(scores - row_max[..., None])
    row_sum = lax.optimization_barrier(jnp.sum(weights, -1))
    rounded = lax.optimization_barrier(weights.astype(jnp.bfloat16)).astype(jnp.float32)
    weighted = jnp.einsum('hrk,hkd->hrd', rounded, value_rows.astype(jnp.float32))
    return (weighted / row_sum[..., None], row_max + jnp.log(row_sum))

def class_attention(query_rows, key_value):
    tile_count, tokens, two_parts, head_count, head_size = key_value.shape
    queries = query_rows.reshape(tile_count, head_count, head_size).astype(jnp.float32)
    scores = jnp.einsum('bhd,bphd->bhp', queries, key_value[:, :, 0].astype(jnp.float32)) / math.sqrt(head_size)
    row_max = lax.optimization_barrier(jnp.max(scores, -1))
    weights = jnp.exp(scores - row_max[..., None])
    row_sum = lax.optimization_barrier(jnp.sum(weights, -1))
    rounded = lax.optimization_barrier(weights.astype(jnp.bfloat16)).astype(jnp.float32)
    weighted = jnp.einsum('bhp,bphd->bhd', rounded, key_value[:, :, 1].astype(jnp.float32))
    return (weighted / row_sum[..., None]).reshape(tile_count, head_count * head_size).astype(jnp.bfloat16)

def encode_block(tile_block, gain_tile, w_kv, w_q, w_to, gain_final, w_proj):
    tile_count, tokens, model_width = tile_block.shape
    normed = normalize(tile_block.astype(jnp.float32), gain_tile.astype(jnp.float32)).astype(jnp.bfloat16)
    key_value = jnp.dot(normed.reshape(tile_count * tokens, model_width), w_kv, preferred_element_type=jnp.float32)
    key_value = key_value.astype(jnp.bfloat16).reshape(tile_count, tokens, 2, model_width // HEAD_T, HEAD_T)
    query_rows = jnp.dot(normed[:, 0], w_q, preferred_element_type=jnp.float32).astype(jnp.bfloat16)
    context = class_attention(query_rows, key_value)
    resid = tile_block[:, 0].astype(jnp.float32) + jnp.dot(context, w_to, preferred_element_type=jnp.float32)
    final = normalize(resid, gain_final.astype(jnp.float32)).astype(jnp.bfloat16)
    return jnp.dot(final, w_proj, preferred_element_type=jnp.float32).astype(jnp.bfloat16)

def merge_branches(local_out, local_log, far_out, far_log):
    length, head_count, head_size = local_out.shape
    offsets = jnp.arange(head_count) % RATE
    chosen = jnp.arange(RATE)[:, None] == offsets[None, :]
    far_full = far_out.transpose(1, 0, 2)[:, None] * chosen[None, :, :, None].astype(far_out.dtype)
    far_full = far_full.reshape(length, head_count, head_size)
    far_logs = jnp.where(chosen[None], far_log.T[:, None, :], masked).reshape(length, head_count)
    upper = jnp.maximum(local_log, far_logs)
    near_weight = jnp.exp(local_log - upper)
    far_weight = jnp.exp(far_logs - upper)
    mixed = (near_weight[..., None] * local_out + far_weight[..., None] * far_full) / (near_weight + far_weight)[..., None]
    return mixed.astype(jnp.bfloat16).reshape(length, head_count * head_size)

def slide_layer(sequence, is_live, gain_slide, w_slide_qkv, w_slide_out):
    length = sequence.shape[0]
    head_size = E // HEADS_S
    score_scale = 1.0 / math.sqrt(head_size)
    slide_normed = normalize(sequence.astype(jnp.float32), gain_slide.astype(jnp.float32)).astype(jnp.bfloat16)
    slide_qkv = jnp.dot(slide_normed, w_slide_qkv, preferred_element_type=jnp.float32).astype(jnp.bfloat16)
    slide_qkv = slide_qkv.reshape(length, 3, HEADS_S, head_size)

    def local_segment(inputs):
        segment, seg_live = inputs
        pieces_out, logs_out = ([], [])
        for group_start in range(0, HEADS_S, head_group):
            part = segment[:, :, group_start:group_start + head_group].transpose(1, 2, 0, 3)
            flags = jnp.broadcast_to(seg_live[None, :], (head_group, SEG))
            result, logs = attend(part[0], part[1], part[2], flags, score_scale)
            pieces_out.append(result)
            logs_out.append(logs)
        return (jnp.concatenate(pieces_out, 0).transpose(1, 0, 2), jnp.concatenate(logs_out, 0).T)
    local_out, local_log = lax.map(local_segment, (slide_qkv.reshape(length // SEG, SEG, 3, HEADS_S, head_size), is_live.reshape(length // SEG, SEG)))
    local_out = local_out.reshape(length, HEADS_S, head_size)
    local_log = local_log.reshape(length, HEADS_S)
    offsets = jnp.arange(HEADS_S) % RATE
    sparse = slide_qkv.reshape(length // RATE, RATE, 3, HEADS_S, head_size).transpose(1, 3, 2, 0, 4)[offsets, jnp.arange(HEADS_S)]
    sparse_live = is_live.reshape(length // RATE, RATE).T[offsets]

    def far_head(inputs):
        queries, key_rows, value_rows, flags = inputs
        result, logs = attend(queries[None], key_rows[None], value_rows[None], flags[None], score_scale)
        return (result[0], logs[0])
    far_out, far_log = lax.map(far_head, (sparse[:, 0], sparse[:, 1], sparse[:, 2], sparse_live))
    mixed = merge_branches(local_out, local_log, far_out, far_log)
    result = sequence.astype(jnp.float32) + jnp.dot(mixed, w_slide_out, preferred_element_type=jnp.float32)
    return jnp.where(is_live[:, None], result, 0.0).astype(jnp.bfloat16)

def reference(patches, gain_tile, w_kv, w_q, w_to, gain_final, w_proj, positions, counts, cache, gain_slide, w_slide_qkv, w_slide_out):
    blocks = patches.reshape(TILES // TILE_DEV, TILE_DEV, P_SIZE, W)
    new_embed = lax.map(lambda tile_block: encode_block(tile_block, gain_tile, w_kv, w_q, w_to, gain_final, w_proj), blocks)
    new_embed = new_embed.reshape(TILES, E)
    results = []
    for slide in range(SLIDES):
        places = positions[slide * NEW_SLIDE:(slide + 1) * NEW_SLIDE]
        sequence = cache[slide].at[places].set(new_embed[slide * NEW_SLIDE:(slide + 1) * NEW_SLIDE])
        is_live = jnp.arange(SLIDE_LEN) < counts[slide]
        results.append(slide_layer(sequence, is_live, gain_slide, w_slide_qkv, w_slide_out))
    return jnp.stack(results)
```

```python
import math
import jax
import jax.numpy as jnp
from jax import lax
from jax.experimental import pallas as pl
from jax.experimental.pallas import tpu as pltpu
from jax.sharding import PartitionSpec as P

MESH = pl.DeviceIdType.MESH
BF = jnp.bfloat16
F32 = jnp.float32
W = 1536
TOK = 256
NP = 32
NT = (((1,), (1,)), ((), ()))


def iota(shape, dim):
    return lax.broadcasted_iota(jnp.int32, shape, dim)


def onehot(cond):
    return jnp.where(cond, 1.0, 0.0).astype(BF)


def mm(a, b):
    return jnp.dot(a, b, preferred_element_type=F32)


def mm_nt(a, b):
    return lax.dot_general(a, b, NT, preferred_element_type=F32)


def norm_rows(x, gain, width):
    mean = jnp.sum(x, -1, keepdims=True) * (1.0 / width)
    c = x - mean
    var = jnp.sum(c * c, -1, keepdims=True) * (1.0 / width)
    return c * lax.rsqrt(var + 1e-6) * gain


def t_kernel(
    patches_ref, gt_ref, kv_ref, q_ref, to_ref, gf_ref, proj_ref, emb_ref,
    send_w, send_kv, wbuf, kbuf, vbuf, wpad, normed, send_cls, clsbuf, scr, usend, ubuf, zsend, zbuf,
    csend, cbuf, rsend, rbuf, esend, ebuf, gain_pad, w_sem, k_sem, v_sem, ws_sem, rsem, ssem,
):
    z = lax.axis_index("fsdp")
    s = lax.axis_index("seq")
    barrier = pltpu.get_barrier_semaphore()

    def greet(zs, ss):
        @pl.when(zs != z)
        def _():
            pl.semaphore_signal(barrier, inc=1, device_id=(zs, ss), device_id_type=MESH)

    def greet_plane(d, _):
        pl.semaphore_signal(barrier, inc=1, device_id=(z, lax.rem(s + d, NP)), device_id_type=MESH)
        return 0

    lax.fori_loop(1, NP, greet_plane, 0)
    for m in range(4):
        greet(s // 8, 4 * lax.rem(s, 8) + m)
    for m in range(2):
        greet(s // 16, 2 * lax.rem(s, 16) + m)
        greet(2 + s // 16, 2 * lax.rem(s, 16) + m)

    r32 = iota((32, 12), 0)
    c32 = iota((32, 12), 1)
    send_w[...] = (
        mm(onehot(r32 == c32), q_ref[...])
        + mm(onehot(r32 == c32 + 12), to_ref[...])
        + mm(onehot(iota((32, 6), 0) == iota((32, 6), 1) + 24), proj_ref[...])
    ).astype(BF)
    send_kv[...] = mm(onehot(iota((32, 24), 0) == iota((32, 24), 1)), kv_ref[...]).astype(BF)
    gain_t = gt_ref[...]
    top = patches_ref[0, 0:16, :].astype(F32)
    ncls = norm_rows(top, gain_t, W)[0:1]
    pair = jnp.concatenate([ncls, top[0:1]], 0)
    send_cls[...] = pair.astype(BF)
    clsbuf[s] = pair.astype(BF)

    pl.semaphore_wait(barrier, NP - 1 + 6)

    def gather_round(src_of, buf, r):
        def one(d, _):
            peer = lax.rem(s + d, NP)
            pltpu.make_async_remote_copy(
                src_ref=src_of(peer), dst_ref=buf.at[s], send_sem=ssem.at[r], recv_sem=rsem.at[r],
                device_id=(z, peer), device_id_type=MESH,
            ).start()
            return 0
        lax.fori_loop(1, NP, one, 0)

    def wait_round(buf, r):
        part = buf.at[pl.ds(0, NP - 1)]
        pltpu.make_async_copy(part, part, rsem.at[r]).wait()

    def drain_round(buf, r):
        part = buf.at[pl.ds(0, NP - 1)]
        pltpu.make_async_copy(part, part, ssem.at[r]).wait()

    gather_round(lambda peer: send_cls, clsbuf, 0)

    def send_to(src, dst, zd, sd, sem, out_sem):
        mine = jnp.logical_and(zd == z, sd == s)

        @pl.when(mine)
        def _():
            pltpu.make_async_copy(src, dst, sem).start()

        @pl.when(jnp.logical_not(mine))
        def _():
            pltpu.make_async_remote_copy(
                src_ref=src, dst_ref=dst, send_sem=out_sem, recv_sem=sem, device_id=(zd, sd), device_id_type=MESH
            ).start()

    for d in range(4):
        zd = lax.rem(z + d, 4)
        send_to(send_w, wbuf.at[lax.rem(s, 4)], zd, 8 * z + s // 4, w_sem, ws_sem)
    sk = 16 * lax.rem(z, 2) + s // 2

    @pl.when(z < 2)
    def _():
        for d in range(4):
            send_to(send_kv, kbuf.at[lax.rem(s, 2)], lax.rem(z + d, 4), sk, k_sem, ws_sem)

    @pl.when(z >= 2)
    def _():
        for d in range(4):
            send_to(send_kv, vbuf.at[lax.rem(s, 2)], lax.rem(z + d, 4), sk, v_sem, ws_sem)

    def norm_block(i, _):
        rows = pl.ds(pl.multiple_of(i * 32, 32), 32)
        normed[rows, :] = norm_rows(patches_ref[0, rows, :].astype(F32), gain_t, W).astype(BF)
        return 0

    lax.fori_loop(0, TOK // 32, norm_block, 0)

    spread = onehot(
        iota((384, 512), 1) == 32 * (iota((384, 512), 0) // 24) + lax.rem(iota((384, 512), 0), 24)
    )
    gain_pad[...] = jnp.concatenate(
        [
            jnp.dot(gf_ref[:, 384 * g : 384 * g + 384], spread.astype(F32), preferred_element_type=F32,
                    precision=lax.Precision.HIGHEST)
            for g in range(4)
        ],
        1,
    )

    r = lax.rem(s, 4)
    wait_round(clsbuf, 0)
    pltpu.make_async_copy(wbuf, wbuf, w_sem).wait()

    def unpack(buf):
        for t in range(NP):
            scr[2 * t : 2 * t + 2, :] = buf[t].astype(F32)
        return scr[...].astype(BF)

    def pack(value, send, own):
        scr[...] = value
        for t in range(NP):
            send[t] = scr[2 * t : 2 * t + 2, :].astype(BF)
        own[s] = send[s]

    cls2 = unpack(clsbuf)
    wall = wbuf[...].reshape(128, W)
    q_all = mm_nt(cls2, wall).astype(BF)
    lane = iota((128, 64), 0)
    krow = iota((128, 64), 1)
    to_k = onehot(
        (12 * (lane // 32) + lax.rem(lane, 32) == 24 * (krow // 32) + lax.rem(krow, 32))
        & (lax.rem(lane, 32) < 12)
        & (lax.rem(krow, 32) < 24)
    )
    q_k = mm(q_all, to_k).astype(BF)
    both = onehot(iota((64, 64), 1) == 2 * (iota((64, 64), 0) // 2))
    q_both = mm(both, q_k)
    col = iota((64, 64), 1)
    j = 24 * (col // 32) + lax.rem(col, 32)
    slot = (48 * r + j) // 64 - (r - 1)
    slot_ok = (lax.rem(iota((64, 64), 0), 2) == slot) & (lax.rem(col, 32) < 24)
    q_exp = jnp.where(slot_ok, q_both, 0.0).astype(BF)
    pltpu.make_async_copy(kbuf, kbuf, k_sem).wait()
    u = mm(q_exp, kbuf[...].reshape(64, W))
    pack(u, usend, ubuf)
    gather_round(lambda peer: usend.at[peer], ubuf, 1)

    raw = mm(onehot(iota((32, 64), 1) == 2 * iota((32, 64), 0) + 1), cls2).astype(BF)
    kk = iota((W, 128), 0)
    ll = iota((W, 128), 1)
    pick = onehot((kk == 48 * s + 12 * (ll // 32) + lax.rem(ll, 32) - 12) & (lax.rem(ll, 32) >= 12) & (lax.rem(ll, 32) < 24))
    raw_cols = mm(raw, pick)
    for g in range(4):
        wpad[:, 512 * g : 512 * g + 512] = mm(wall[:, 384 * g : 384 * g + 384], spread).astype(BF)

    wait_round(ubuf, 1)
    u2 = unpack(ubuf)
    parts = mm_nt(u2, normed[...])

    def head_of(row):
        src = row // 2
        return 3 * (src // 4) + lax.rem(src, 4) - 1 + lax.rem(row, 2)

    def real(row):
        a = lax.rem(row, 8)
        return (a != 0) & (a != 7)

    ra = iota((64, 64), 0)
    rb = iota((64, 64), 1)
    join = jnp.where((head_of(ra) == head_of(rb)) & real(rb), 1.0, 0.0)
    scores = jnp.dot(join, parts, preferred_element_type=F32, precision=lax.Precision.HIGHEST) * 0.125
    mx = jnp.max(scores, -1, keepdims=True)
    wts = jnp.exp(scores - mx)
    tot = jnp.sum(wts, -1, keepdims=True)
    zz = mm(wts.astype(BF), normed[...]) / tot
    pack(zz, zsend, zbuf)
    gather_round(lambda peer: zsend.at[peer], zbuf, 2)

    pltpu.make_async_copy(vbuf, vbuf, v_sem).wait()
    wait_round(zbuf, 2)
    z2 = unpack(zbuf)
    ctx2 = jnp.where(slot_ok, mm_nt(z2, vbuf[...].reshape(64, W)), 0.0).astype(BF)
    fold = onehot(iota((32, 64), 1) // 2 == iota((32, 64), 0))
    ctx = mm(fold, ctx2).astype(BF)
    half = 64 * lax.rem(s, 2)
    place = onehot(iota((64, 128), 1) == iota((64, 128), 0) + half)
    csend[...] = mm(ctx, place).astype(BF)
    cbuf[s] = csend[...]
    gather_round(lambda peer: csend, cbuf, 3)

    def lanes2(buf):
        return jnp.concatenate([buf[2 * a] + buf[2 * a + 1] for a in range(16)], 1)

    wait_round(cbuf, 3)
    resid = mm_nt(lanes2(cbuf), wpad[...]) + raw_cols
    la = iota((128, 128), 0)
    lb = iota((128, 128), 1)
    ca = lax.rem(la, 32) - 12
    place_r = onehot((lb == half + 32 * (la // 64) + 12 * lax.rem(la // 32, 2) + ca) & (ca >= 0) & (ca < 12))
    rsend[...] = mm(resid.astype(BF), place_r).astype(BF)
    rbuf[s] = rsend[...]
    gather_round(lambda peer: rsend, rbuf, 4)

    wait_round(rbuf, 4)
    full = lanes2(rbuf).astype(F32)
    valid = lax.rem(iota((1, 2048), 1), 32) < 24
    mean = jnp.sum(full, -1, keepdims=True) * (1.0 / W)
    cen = jnp.where(valid, full - mean, 0.0)
    var = jnp.sum(cen * cen, -1, keepdims=True) * (1.0 / W)
    final = (cen * lax.rsqrt(var + 1e-6) * gain_pad[...]).astype(BF)
    emb = mm_nt(final, wpad[...]).astype(BF)
    ce = lax.rem(la, 32) - 24
    place_e = onehot((lb == 32 * lax.rem(s, 4) + 6 * (la // 32) + ce) & (ce >= 0) & (ce < 6))
    esend[...] = mm(emb, place_e).astype(BF)
    ebuf[s] = esend[...]
    gather_round(lambda peer: esend, ebuf, 5)

    wait_round(ebuf, 5)
    wide = jnp.concatenate([(ebuf[4 * a] + ebuf[4 * a + 1]) + (ebuf[4 * a + 2] + ebuf[4 * a + 3]) for a in range(8)], 1)
    for g in range(2):
        emb_ref[:, 384 * g : 384 * g + 384] = mm_nt(wide[:, 512 * g : 512 * g + 512], spread).astype(BF)

    drain_round(clsbuf, 0)
    drain_round(ubuf, 1)
    drain_round(zbuf, 2)
    drain_round(cbuf, 3)
    drain_round(rbuf, 4)
    drain_round(ebuf, 5)
    mine_w = (s == 8 * z + s // 4)
    mine_k = (s == sk)
    three = wbuf.at[pl.ds(0, 3)]
    pltpu.make_async_copy(three, three, ws_sem).wait()
    pltpu.make_async_copy(three, three, ws_sem).wait()

    @pl.when(jnp.logical_not(mine_w))
    def _():
        pltpu.make_async_copy(send_w, send_w, ws_sem).wait()

    @pl.when(jnp.logical_not(mine_k))
    def _():
        pltpu.make_async_copy(send_kv, send_kv, ws_sem).wait()


def t_scratch():
    V = pltpu.VMEM
    return [
        V((32, W), BF), V((32, W), BF), V((4, 32, W), BF), V((2, 32, W), BF), V((2, 32, W), BF), V((128, 2048), BF),
        V((TOK, W), BF), V((2, W), BF), V((NP, 2, W), BF), V((64, W), F32),
        V((NP, 2, W), BF), V((NP, 2, W), BF), V((NP, 2, W), BF), V((NP, 2, W), BF),
        V((32, 128), BF), V((NP, 32, 128), BF), V((32, 128), BF), V((NP, 32, 128), BF), V((32, 128), BF), V((NP, 32, 128), BF),
        V((1, 2048), F32),
        pltpu.SemaphoreType.DMA, pltpu.SemaphoreType.DMA, pltpu.SemaphoreType.DMA, pltpu.SemaphoreType.DMA,
        pltpu.SemaphoreType.DMA((6,)), pltpu.SemaphoreType.DMA((6,)),
    ]


def tile_embeddings(patches, gain_tile, w_kv, w_q, w_to, gain_final, w_proj):
    vm = pl.BlockSpec(memory_space=pltpu.VMEM)
    return pl.pallas_call(
        t_kernel,
        out_shape=jax.ShapeDtypeStruct((NP, 768), BF),
        in_specs=[vm] * 7,
        out_specs=vm,
        scratch_shapes=t_scratch(),
        compiler_params=pltpu.CompilerParams(collective_id=0, has_side_effects=True, vmem_limit_bytes=40 << 20),
    )(patches, gain_tile.reshape(1, W), w_kv.T, w_q.T, w_to.T, gain_final.reshape(1, W), w_proj.T)


HEAD_T = 64
E = 768
HEADS_S = 16
SEG = 1024
RATE = 16


epsilon = 1e-06
masked = -1e30
head_group = 4


def normalize(values, gain_vec):
    row_mean = jnp.mean(values, -1, keepdims=True)
    centered = values - row_mean
    variance = jnp.mean(centered * centered, -1, keepdims=True)
    return centered * lax.rsqrt(variance + epsilon) * gain_vec


def attend(queries, key_rows, value_rows, key_live, score_scale):
    scores = (
        jnp.einsum("hrd,hkd->hrk", queries, key_rows, preferred_element_type=jnp.float32)
        * score_scale
    )
    scores = jnp.where(key_live[:, None, :], scores, masked)
    row_max = jnp.max(scores, -1)
    weights = jnp.exp(scores - row_max[..., None])
    row_sum = jnp.sum(weights, -1)
    weighted = jnp.einsum(
        "hrk,hkd->hrd", weights.astype(jnp.bfloat16), value_rows, preferred_element_type=jnp.float32
    )
    return (weighted / row_sum[..., None], row_max + jnp.log(row_sum))


def merge_branches(local_out, local_log, far_out, far_log):
    length, head_count, head_size = local_out.shape
    offsets = jnp.arange(head_count) % RATE
    chosen = jnp.arange(RATE)[:, None] == offsets[None, :]
    far_full = far_out.transpose(1, 0, 2)[:, None] * chosen[None, :, :, None].astype(far_out.dtype)
    far_full = far_full.reshape(length, head_count, head_size)
    far_logs = jnp.where(chosen[None], far_log.T[:, None, :], masked).reshape(length, head_count)
    upper = jnp.maximum(local_log, far_logs)
    near_weight = jnp.exp(local_log - upper)
    far_weight = jnp.exp(far_logs - upper)
    mixed = (near_weight[..., None] * local_out + far_weight[..., None] * far_full) / (
        near_weight + far_weight
    )[..., None]
    return mixed.astype(jnp.bfloat16).reshape(length, head_count * head_size)


def per_device(
    patches,
    gain_tile,
    w_kv,
    w_q,
    w_to,
    gain_final,
    w_proj,
    positions,
    counts,
    cache,
    gain_slide,
    w_slide_qkv,
    w_slide_out,
):
    new_embed = tile_embeddings(patches, gain_tile, w_kv, w_q, w_to, gain_final, w_proj)
    rows_dev = cache.shape[1]
    arrivals = new_embed
    row_ids = lax.axis_index("seq") * rows_dev + jnp.arange(rows_dev, dtype=jnp.int32)
    matches = positions[None, :] == row_ids[:, None]
    placed = jnp.dot(
        matches.astype(jnp.bfloat16), arrivals, preferred_element_type=jnp.float32
    ).astype(jnp.bfloat16)
    sequence = jnp.where(jnp.any(matches, 1)[:, None], placed, cache[0])
    limit = counts[0]
    is_live = row_ids < limit
    head_size = E // HEADS_S
    score_scale = 1.0 / math.sqrt(head_size)
    slide_normed = normalize(sequence.astype(jnp.float32), gain_slide).astype(jnp.bfloat16)
    slide_qkv = jnp.dot(slide_normed, w_slide_qkv, preferred_element_type=jnp.float32).astype(
        jnp.bfloat16
    )
    slide_qkv = slide_qkv.reshape(rows_dev, 3, HEADS_S, head_size)

    def local_segment(inputs):
        segment, seg_live = inputs
        pieces_out, logs_out = ([], [])
        for group_start in range(0, HEADS_S, head_group):
            part = segment[:, :, group_start : group_start + head_group].transpose(1, 2, 0, 3)
            flags = jnp.broadcast_to(seg_live[None, :], (head_group, SEG))
            result, logs = attend(part[0], part[1], part[2], flags, score_scale)
            pieces_out.append(result)
            logs_out.append(logs)
        return (jnp.concatenate(pieces_out, 0).transpose(1, 0, 2), jnp.concatenate(logs_out, 0).T)

    local_out, local_log = lax.map(
        local_segment,
        (
            slide_qkv.reshape(rows_dev // SEG, SEG, 3, HEADS_S, head_size),
            is_live.reshape(rows_dev // SEG, SEG),
        ),
    )
    local_out = local_out.reshape(rows_dev, HEADS_S, head_size)
    local_log = local_log.reshape(rows_dev, HEADS_S)
    sparse_rows = rows_dev // RATE
    offsets = jnp.arange(HEADS_S, dtype=jnp.int32) % RATE
    sparse = slide_qkv.reshape(sparse_rows, RATE, 3, HEADS_S, head_size).transpose(1, 3, 2, 0, 4)[
        offsets, jnp.arange(HEADS_S)
    ]
    far_query = sparse[:, 0]
    far_keys = sparse[:, 1]
    far_values = sparse[:, 2]
    start_state = jnp.concatenate(
        [
            jnp.zeros((HEADS_S, sparse_rows, head_size), jnp.float32),
            jnp.full((HEADS_S, sparse_rows, 1), masked, jnp.float32),
            jnp.zeros((HEADS_S, sparse_rows, 1), jnp.float32),
        ],
        -1,
    )
    stacked = jnp.stack([far_keys, far_values], 0)
    shard_piece = lax.all_gather(stacked, "seq", axis=2, tiled=True)
    weighted = start_state[..., :head_size]
    running_max = start_state[..., head_size]
    running_sum = start_state[..., head_size + 1]
    key_rows = shard_piece[0]
    value_rows = shard_piece[1]
    width_now = key_rows.shape[1]
    key_pos = jnp.arange(width_now, dtype=jnp.int32)[None, :] * RATE + offsets[:, None]
    scores = (
        jnp.einsum("hrd,hkd->hrk", far_query, key_rows, preferred_element_type=jnp.float32)
        * score_scale
    )
    scores = jnp.where((key_pos < limit)[:, None, :], scores, masked)
    new_max = jnp.maximum(running_max, jnp.max(scores, -1))
    rescale = jnp.exp(running_max - new_max)
    weights = jnp.exp(scores - new_max[..., None])
    running_sum = running_sum * rescale + jnp.sum(weights, -1)
    weighted = weighted * rescale[..., None] + jnp.einsum(
        "hrk,hkd->hrd", weights.astype(jnp.bfloat16), value_rows, preferred_element_type=jnp.float32
    )
    folded = jnp.concatenate([weighted, new_max[..., None], running_sum[..., None]], -1)
    final_sum = folded[..., head_size + 1]
    far_out = folded[..., :head_size] / final_sum[..., None]
    far_log = folded[..., head_size] + jnp.log(final_sum)
    mixed = merge_branches(local_out, local_log, far_out, far_log)
    result = sequence.astype(jnp.float32) + jnp.dot(
        mixed, w_slide_out, preferred_element_type=jnp.float32
    )
    return jnp.where(is_live[:, None], result, 0.0).astype(jnp.bfloat16)[None]


def solution(mesh):
    placed = (
        P(("fsdp", "seq"), None, None),
        P(),
        P(None, ("fsdp", "seq")),
        P(None, ("fsdp", "seq")),
        P(None, ("fsdp", "seq")),
        P(),
        P(None, ("fsdp", "seq")),
        P("fsdp"),
        P("fsdp"),
        P("fsdp", "seq", None),
        P(),
        P(),
        P(),
    )
    return jax.shard_map(
        per_device, mesh=mesh, in_specs=placed, out_specs=P("fsdp", "seq", None), check_vma=False
    )
```
